1024 devices in a mesh: member: 32 (over z), sx: 4 (over y_lo, core), sy: 8 (over x, y_hi).
Axes of the slice: x: 4, y: 4 (y_hi: 2, y_lo: 2; y = y_hi * 2 + y_lo), z: 32, core: 2. Of those that a mesh axis runs over, the one named last changes fastest.
Arguments:
- anomalies: bfloat16 [256, 3, 16, 128, 128], P('member', None, 'sx', 'sy'), may hold values from -6 to 6
- sigma: float32 [16, 128, 128], P('sx', 'sy'), may hold values from 0.5 to 2
- taper_x: float32 [16, 7], replicated, may hold values from 0.05 to 1
- taper_y: float32 [128, 7], replicated, may hold values from 0.05 to 1
- taper_z: float32 [128, 128], replicated, may hold values from -0.07 to 1.07
- innovation: float32 [4, 8, 2048], P('sx', 'sy'), may hold values from -6 to 6
- obs_inverse: float32 [4, 8, 2048], P('sx', 'sy'), may hold values from 0.25 to 4
- obs_index: int32 [4, 8, 2048], P('sx', 'sy'), may hold values from 0 to 8191
- obs_slot: int32 [4, 8, 2048], P('sx', 'sy'), may hold values from 0 to 2
Outputs:
- alpha_weights: float32 [256, 16, 128, 128], P('member', 'sx', 'sy')
- static_control: float32 [16, 128, 128], P('sx', 'sy')
- increment: float32 [3, 16, 128, 128], P(None, 'sx', 'sy')
The draws below stay inside these ranges and needn't reach their ends.
All inputs are finite; a program needn't handle non-finite values.
Results may differ from the reference program's by a relative error of at most 0.001.
Values sent between devices are 32-bit elements; how exact they have to be, the bound alone decides.
No kernel may reach another device: no remote copies, remote signals or barrier semaphores. Data moves between devices by JAX's collectives and lax.ppermute only.
A program may use at most 32 MiB of HBM per device.

```python
import math
import jax
import jax.numpy as jnp
from jax import lax

MEMBERS = 256
SLOTS = 3
LEV = 128
HW = 3
ITERS = 2
CX = 4
CY = 16
OBS_DEV = 2048
NX = 16
NY = 128
N_SX = 4
N_SY = 8


def band_table(key, count):
    upper = jax.random.uniform(key, (count + HW, HW), jnp.float32, 0.05, 0.3)
    centre = jax.random.uniform(jax.random.fold_in(key, 7), (count,), jnp.float32, 0.6, 1.0)
    columns = []
    for offset in range(-HW, HW + 1):
        if offset == 0:
            columns.append(centre)
        elif offset > 0:
            columns.append(upper[HW:HW + count, offset - 1])
        else:
            columns.append(upper[HW + offset:HW + offset + count, -offset - 1])
    return jnp.stack(columns, axis=1)


def draw_taper_x(key, part):
    key = jax.random.fold_in(key, 1)
    return band_table(key, NX)


def draw_taper_y(key, part):
    key = jax.random.fold_in(key, 2)
    return band_table(key, NY)


def draw_taper_z(key, part):
    key = jax.random.fold_in(key, 3)
    spread = jax.random.uniform(key, (LEV, LEV), jnp.float32, -0.07, 0.07)
    centre = jax.random.uniform(jax.random.fold_in(key, 5), (LEV,), jnp.float32, 0.7, 1.0)
    return 0.5 * (spread + spread.T) + jnp.diag(centre)


def with_ends(entries, own_key, low, high):
    extent = entries.shape
    spot = [jax.random.randint(jax.random.fold_in(own_key, axis), (), 0, extent[axis]) for axis in range(len(extent))]
    entries = entries.at[tuple(spot)].set(low)
    longest = extent.index(max(extent))
    spot[longest] = (spot[longest] + 1) % extent[longest]
    return entries.at[tuple(spot)].set(high)


def block_levels(stream_key, extent, cuts, low, top_value):
    gain = 1.0
    for dim, shards_of in cuts:
        heights = jax.random.uniform(jax.random.fold_in(jax.random.fold_in(stream_key, 6), dim), (shards_of,), jnp.float32, low / len(cuts), top_value / len(cuts))
        gain = gain * jnp.repeat(jnp.exp(heights), extent[dim] // shards_of).reshape((-1,) + (1,) * (len(extent) - 1 - dim))
    return gain


def scatter_about(key, extent, scale, bound, cuts=(), held_as=jnp.bfloat16):
    loudness = block_levels(key, extent, cuts, -0.22, 0.18) if cuts else 1.0
    result = jax.random.normal(key, extent, jnp.float32) * scale * loudness
    return jnp.minimum(jnp.maximum(result, -bound), bound).astype(held_as)


def setup_inputs(seed: int = 0) -> dict:
    keys = jax.random.split(jax.random.key(seed), 10)
    anomalies = scatter_about(keys[0], (MEMBERS, SLOTS, NX, NY, LEV), 1.0, 6.0, ((0, 32), (2, 4), (3, 8)))
    sigma = jnp.clip(jnp.exp(math.log(2.0) - 1.3862944 * jax.random.uniform(keys[1], (NX, NY, LEV), jnp.float32) ** block_levels(keys[1], (NX, NY, LEV), ((0, 4), (1, 8)), -0.2, 0.2)), 0.5, 2.0)
    taper_x = draw_taper_x(jax.random.fold_in(keys[9], 71), 0)
    taper_y = draw_taper_y(jax.random.fold_in(keys[9], 71), 0)
    taper_z = draw_taper_z(jax.random.fold_in(keys[9], 71), 0)
    innovation = scatter_about(keys[5], (N_SX, N_SY, OBS_DEV), 1.0, 6.0, ((0, 4), (1, 8)), jnp.float32)
    obs_inverse = jnp.clip(jnp.exp(math.log(4.0) - 2.7725887 * jax.random.uniform(keys[6], (N_SX, N_SY, OBS_DEV), jnp.float32) ** block_levels(keys[6], (N_SX, N_SY, OBS_DEV), ((0, 4), (1, 8)), -0.2, 0.2)), 0.25, 4.0)
    obs_index = with_ends(jax.random.randint(keys[7], (N_SX, N_SY, OBS_DEV), 0, CX * CY * LEV), jax.random.fold_in(keys[7], 1), 0, (CX * CY * LEV) - 1).astype(jnp.int32)
    obs_slot = with_ends(jax.random.randint(keys[8], (N_SX, N_SY, OBS_DEV), 0, SLOTS), jax.random.fold_in(keys[8], 1), 0, SLOTS - 1).astype(jnp.int32)
    return {"anomalies": anomalies, "sigma": sigma, "taper_x": taper_x, "taper_y": taper_y, "taper_z": taper_z, "innovation": innovation, "obs_inverse": obs_inverse, "obs_index": obs_index, "obs_slot": obs_slot}


STATIC_WEIGHT = 0.6

def reference(anomalies, sigma, taper_x, taper_y, taper_z, innovation, obs_inverse, obs_index, obs_slot):
    ens_weight = 0.8 / math.sqrt(MEMBERS - 1)

    def smooth_one(field):
        padded = jnp.pad(field, ((HW, HW), (0, 0), (0, 0)))
        along_x = jnp.zeros((NX, NY, LEV), jnp.float32)
        for offset in range(2 * HW + 1):
            along_x = along_x + taper_x[:, offset][:, None, None] * padded[offset:offset + NX]
        padded = jnp.pad(along_x, ((0, 0), (HW, HW), (0, 0)))
        along_y = jnp.zeros((NX, NY, LEV), jnp.float32)
        for offset in range(2 * HW + 1):
            along_y = along_y + taper_y[:, offset][None, :, None] * padded[:, offset:offset + NY]
        return jnp.einsum('xyk,kl->xyl', along_y, taper_z, precision=lax.Precision.HIGHEST)
    region_x = jnp.arange(N_SX, dtype=jnp.int32)[:, None, None]
    region_y = jnp.arange(N_SY, dtype=jnp.int32)[None, :, None]

    def blocks(field):
        shaped = field.reshape(SLOTS, N_SX, CX, N_SY, CY, LEV).transpose(0, 1, 3, 2, 4, 5)
        return shaped.reshape(SLOTS, N_SX, N_SY, CX * CY * LEV)

    def sample(field):
        return blocks(field)[obs_slot, region_x, region_y, obs_index]

    def spread(values):
        grid = jnp.zeros((SLOTS, N_SX, N_SY, CX * CY * LEV), jnp.float32)
        grid = grid.at[obs_slot, region_x, region_y, obs_index].add(values)
        grid = grid.reshape(SLOTS, N_SX, N_SY, CX, CY, LEV).transpose(0, 1, 3, 2, 4, 5)
        return grid.reshape(SLOTS, NX, NY, LEV)

    def forward(control):

        def member_term(total, pair):
            anomaly, weights = pair
            return (total + anomaly.astype(jnp.float32) * smooth_one(weights)[None], None)
        ens_total, _ = lax.scan(member_term, jnp.zeros((SLOTS, NX, NY, LEV), jnp.float32), (anomalies, control[0]))
        static = STATIC_WEIGHT * sigma * smooth_one(control[1])
        return static[None] + ens_weight * ens_total

    def adjoint(values):
        grid = spread(values)
        grad_alpha = lax.map(lambda anomaly: smooth_one(ens_weight * lax.optimization_barrier(jnp.sum(anomaly.astype(jnp.float32) * grid, axis=0))), anomalies)
        grad_static = smooth_one(STATIC_WEIGHT * sigma * lax.optimization_barrier(jnp.sum(grid, axis=0)))
        return (grad_alpha, grad_static)

    def apply_system(control):
        field = forward(control)
        grad_alpha, grad_static = adjoint(obs_inverse * sample(field))
        return ((control[0] + grad_alpha, control[1] + grad_static), field)

    def inner(left, right):
        return jnp.sum(left[0] * right[0]) + jnp.sum(left[1] * right[1])

    def combine(first, scale, second):
        return jax.tree.map(lambda left, right: left + scale * right, first, second)
    rhs = adjoint(obs_inverse * innovation)
    solution = jax.tree.map(jnp.zeros_like, rhs)
    residual = rhs
    direction = rhs
    increment = jnp.zeros((SLOTS, NX, NY, LEV), jnp.float32)
    norm_now = inner(residual, residual)
    for step in range(ITERS):
        image, field = apply_system(direction)
        step_size = norm_now / inner(direction, image)
        solution = combine(solution, step_size, direction)
        increment = increment + step_size * field
        if step + 1 < ITERS:
            residual = combine(residual, -step_size, image)
            norm_next = inner(residual, residual)
            direction = combine(residual, norm_next / norm_now, direction)
            norm_now = norm_next
    return (solution[0], solution[1], increment)
```

```python
import functools
import math

import jax
import jax.numpy as jnp
from jax import lax
from jax.experimental import pallas as pl
from jax.experimental.pallas import tpu as pltpu
from jax.sharding import PartitionSpec as P

HW = 3
STATIC_WEIGHT = 0.6
F32 = jnp.float32
BF16 = jnp.bfloat16
HIGH = lax.Precision.HIGH
HIGHEST = lax.Precision.HIGHEST


def halves(value):
    top = value.astype(BF16)
    return top, (value - top.astype(F32)).astype(BF16)


def one_hot(rows, index):
    return lax.broadcasted_iota(jnp.int32, (rows, index.shape[-1]), 0) == index


def spread_kernel(place_ref, weight_ref, grid_ref):
    cells, levels = grid_ref.shape
    at_cell = one_hot(cells, place_ref[0:1, :]).astype(BF16)
    at_level = one_hot(levels, place_ref[1:2, :])
    top, low = halves(jnp.where(at_level, weight_ref[...], 0.0))
    contract = (((1,), (1,)), ((), ()))
    grid_ref[...] = lax.dot_general(
        at_cell, top, contract, preferred_element_type=F32
    ) + lax.dot_general(at_cell, low, contract, preferred_element_type=F32)


def sample_kernel(place_ref, field_ref, value_ref):
    fields, cells, levels = field_ref.shape
    at_cell = one_hot(cells, place_ref[0:1, :]).astype(BF16)
    at_level = one_hot(levels, place_ref[1:2, :])
    contract = (((0,), (0,)), ((), ()))
    for i in range(fields):
        top, low = halves(field_ref[i])
        columns = lax.dot_general(
            top, at_cell, contract, preferred_element_type=F32
        ) + lax.dot_general(low, at_cell, contract, preferred_element_type=F32)
        value_ref[i : i + 1, :] = jnp.sum(jnp.where(at_level, columns, 0.0), axis=0, keepdims=True)


def groups(size, width, stride):
    seen, out = set(), []
    for first in range(size):
        if first not in seen:
            members = [first + stride * k for k in range(width)]
            seen.update(members)
            out.append(members)
    return out


def exchange(blocks, axis, index_groups=None):
    return lax.all_to_all(blocks, axis, 0, 0, axis_index_groups=index_groups, tiled=True)


def gathered(block, width, axis, index_groups=None):
    return exchange(jnp.broadcast_to(block[None], (width,) + block.shape), axis, index_groups)


def neighbours(low_side, high_side, axis):
    count = lax.axis_size(axis)
    up = [(i, i + 1) for i in range(count - 1)]
    down = [(j, i) for i, j in up]
    return lax.ppermute(high_side, axis, up), lax.ppermute(low_side, axis, down)


def taps(field, table, dim, count):
    total = None
    for offset in range(2 * HW + 1):
        shape = [1] * field.ndim
        shape[dim] = count
        term = table[:, offset].reshape(shape) * lax.slice_in_dim(field, offset, offset + count, axis=dim)
        total = term if total is None else total + term
    return total


def flipped(table):
    rows = table.shape[0]
    padded = jnp.pad(table, ((HW, HW), (0, 0)))
    return jnp.stack([padded[o : o + rows, 2 * HW - o] for o in range(2 * HW + 1)], axis=1)


def window(table, axis, count, rim):
    padded = jnp.pad(table, ((rim, rim), (0, 0)))
    return lax.dynamic_slice_in_dim(padded, lax.axis_index(axis) * count, count + 2 * rim, 0)


def body(anomalies, sigma, taper_x, taper_y, taper_z, innovation, obs_inverse, obs_index, obs_slot):
    local_members, slots, cells_x, cells_y, levels = anomalies.shape
    member_devices = lax.axis_size("member")
    ens_weight = 0.8 / math.sqrt(local_members * member_devices - 1)
    share = 1.0 / member_devices
    cells = cells_x * cells_y
    count = obs_index.shape[-1]
    rows = count // levels

    near = 8 if member_devices % 8 == 0 else 1
    far = member_devices // near
    near_groups = groups(member_devices, near, 1)
    far_groups = groups(member_devices, far, near)
    close = 4 if member_devices % 4 == 0 else 1
    wide = member_devices // close
    close_groups = groups(member_devices, close, 1)
    wide_groups = groups(member_devices, wide, close)

    index_flat = obs_index.reshape(1, -1)
    place = jnp.concatenate(
        [obs_slot.reshape(1, -1) * cells + index_flat // levels, index_flat % levels], axis=0
    )
    obs_weight = obs_inverse.reshape(1, -1)
    first_weight = obs_weight * innovation.reshape(1, -1)

    x_rows = window(taper_x, "sx", cells_x, 0)
    x_flip = window(flipped(taper_x), "sx", cells_x, 0)
    y_rows_wide = window(taper_y, "sy", cells_y, HW)
    y_rows = y_rows_wide[HW : HW + cells_y]
    y_flip = window(flipped(taper_y), "sy", cells_y, 0)
    x_pair = jnp.stack([x_rows, x_flip])
    y_pair = jnp.stack([y_rows, y_flip])
    z_pair = jnp.stack([taper_z, taper_z.T])

    def spread(weights):
        return pl.pallas_call(
            spread_kernel,
            out_shape=jax.ShapeDtypeStruct((slots * cells, levels), F32),
            compiler_params=pltpu.CompilerParams(vmem_limit_bytes=32 * 2**20),
        )(place, weights).reshape(slots, cells_x, cells_y, levels)

    def sample(fields):
        return pl.pallas_call(
            sample_kernel,
            out_shape=jax.ShapeDtypeStruct((fields.shape[0], count), F32),
            compiler_params=pltpu.CompilerParams(vmem_limit_bytes=32 * 2**20),
        )(place, fields.reshape(fields.shape[0], slots * cells, levels))

    def apply(weights):
        grid = spread(weights)
        ens_side = ens_weight * jnp.sum(anomalies.astype(F32) * grid[None], axis=1)
        static_side = STATIC_WEIGHT * sigma * jnp.sum(grid, axis=0)
        stack = jnp.concatenate([ens_side, static_side[None]], axis=0)
        left, right = neighbours(stack[:, :, : 2 * HW], stack[:, :, cells_y - 2 * HW :], "sy")
        stack = jnp.concatenate([left, stack, right], axis=2)
        wide_y = cells_y + 2 * HW
        stack = taps(stack, y_rows_wide, 2, wide_y)
        above, below = neighbours(stack[:, :HW], stack[:, cells_x - HW :], "sx")
        stack = taps(jnp.concatenate([above, stack, below], axis=1), x_rows, 1, cells_x)
        stack = jnp.einsum("bxyk,kl->bxyl", stack, taper_z, precision=HIGH)
        control = stack[:, :, HW : HW + cells_y]
        above, below = neighbours(stack[:, :HW], stack[:, cells_x - HW :], "sx")
        stack = jnp.concatenate([above, stack, below], axis=1)
        fields = []
        for which in range(2):
            out = taps(stack, x_pair[which], 1, cells_x)
            out = taps(out, y_pair[which], 2, cells_y)
            out = jnp.einsum("bxyk,kl->bxyl", out, z_pair[which], precision=HIGH)
            ens_part = ens_weight * jnp.sum(anomalies.astype(F32) * out[:-1, None], axis=0)
            fields.append(ens_part + (share * STATIC_WEIGHT) * (sigma * out[-1])[None])
        sampled = sample(jnp.stack(fields)).reshape(2, rows, levels)
        return control, fields[0], sampled

    control0, field0, sampled0 = apply(first_weight)
    part = jnp.sum(gathered(sampled0[0], close, "member", close_groups), axis=0)
    seen0 = jnp.sum(gathered(part, wide, "member", wide_groups), axis=0)
    obs_rows = obs_weight.reshape(rows, levels)
    weight1 = obs_rows * seen0
    control1, field1, sampled1 = apply(weight1.reshape(1, -1))

    flat = jnp.concatenate(
        [
            block.reshape(near, -1, levels)
            for block in (sampled0[1], sampled1[0], sampled1[1], field0, field1)
        ],
        axis=1,
    )
    chunk = jnp.sum(exchange(flat, "member", near_groups), axis=0)
    chunk = jnp.sum(gathered(chunk, far, "member", far_groups), axis=0)
    total = gathered(chunk, near, "member", near_groups)
    obs_chunk = rows // near
    seen = total[:, : 3 * obs_chunk].reshape(near, 3, obs_chunk, levels)
    flip0, seen1, flip1 = (seen[:, i].reshape(rows, levels) for i in range(3))
    fields = total[:, 3 * obs_chunk :].reshape(near, 2, -1, levels)
    total0, total1 = (fields[:, i].reshape(slots, cells_x, cells_y, levels) for i in range(2))

    weight0 = first_weight.reshape(rows, levels)
    weight2 = obs_rows * seen1
    products = jnp.stack(
        [
            jnp.sum(a * b, axis=0)
            for a, b in (
                (weight0, flip0),
                (weight1, flip0),
                (weight1, flip1),
                (weight2, flip0),
                (weight2, flip1),
            )
        ]
    )
    regions = lax.axis_size("sx") * lax.axis_size("sy")
    products = jnp.sum(gathered(products, regions, ("sx", "sy")), axis=(0, 2))
    p00, p01, p11, p02, p12 = (products[i] for i in range(5))

    step0 = p00 / (p00 + p01)
    keep = 1.0 - step0
    next_norm = keep * (keep * p00 - 2.0 * step0 * p01) + step0 * step0 * p11
    beta = next_norm / p00
    lead = keep + beta
    own = lead * (lead * p00 - 2.0 * step0 * p01) + step0 * step0 * p11
    cross = lead * (lead * p01 - step0 * p02) - step0 * (lead * p11 - step0 * p12)
    step1 = next_norm / (own + cross)
    mix0 = step0 + step1 * lead
    mix1 = -step1 * step0
    control = mix0 * control0 + mix1 * control1
    increment = mix0 * total0 + mix1 * total1
    return control[:-1], control[-1], increment


def solution(mesh):
    return jax.shard_map(
        body,
        mesh=mesh,
        in_specs=(
            P("member", None, "sx", "sy", None),
            P("sx", "sy", None),
            P(),
            P(),
            P(),
            P("sx", "sy", None),
            P("sx", "sy", None),
            P("sx", "sy", None),
            P("sx", "sy", None),
        ),
        out_specs=(P("member", "sx", "sy", None), P("sx", "sy", None), P(None, "sx", "sy", None)),
        check_vma=False,
    )
```

```python
import functools
import math

import jax
import jax.numpy as jnp
from jax import lax
from jax.experimental import pallas as pl
from jax.experimental.pallas import tpu as pltpu
from jax.sharding import PartitionSpec as P

HW = 3
STATIC_WEIGHT = 0.6
F32 = jnp.float32
BF16 = jnp.bfloat16
HIGH = lax.Precision.HIGH
HIGHEST = lax.Precision.HIGHEST


def halves(value):
    top = value.astype(BF16)
    return top, (value - top.astype(F32)).astype(BF16)


def one_hot(rows, index):
    return lax.broadcasted_iota(jnp.int32, (rows, index.shape[-1]), 0) == index


def adjoint_kernel(
    ens_weight, cells_y, place_ref, first_ref, second_ref, anomaly_ref, sigma_ref, stack_ref, low_ref, high_ref
):
    members, slots, cells, levels = anomaly_ref.shape
    at_cell = one_hot(slots * cells, place_ref[0:1, :]).astype(BF16)
    at_level = one_hot(levels, place_ref[1:2, :])
    top, low = halves(jnp.where(at_level, first_ref[...] * second_ref[...], 0.0))
    contract = (((1,), (1,)), ((), ()))
    grid = lax.dot_general(at_cell, top, contract, preferred_element_type=F32) + lax.dot_general(
        at_cell, low, contract, preferred_element_type=F32
    )
    parts = [grid[s * cells : (s + 1) * cells] for s in range(slots)]
    weighted = [ens_weight * part for part in parts]

    def put(k, field):
        stack_ref[k] = field
        for x in range(cells // cells_y):
            first, rim = x * cells_y, 2 * HW
            low_ref[k, x * rim : (x + 1) * rim, :] = field[first : first + rim]
            high_ref[k, x * rim : (x + 1) * rim, :] = field[first + cells_y - rim : first + cells_y]

    for k in range(members):
        put(k, sum(anomaly_ref[k, s].astype(F32) * weighted[s] for s in range(slots)))
    put(members, STATIC_WEIGHT * sigma_ref[...] * sum(parts))


def forward_kernel(
    ens_weight,
    share,
    x_ref,
    place_ref,
    above_ref,
    stack_ref,
    below_ref,
    y_ref,
    z_ref,
    anomaly_ref,
    sigma_ref,
    field_ref,
    value_ref,
    wide_ref,
    held_ref,
):
    members, slots, cells, levels = anomaly_ref.shape
    cells_x = stack_ref.shape[1]
    cells_y = cells // cells_x
    rim = above_ref.shape[1]

    def row(x):
        if x < rim:
            return above_ref[:, x]
        if x < rim + cells_x:
            return stack_ref[:, x - rim]
        return below_ref[:, x - rim - cells_x]

    at_cell = one_hot(slots * cells, place_ref[0:1, :]).astype(BF16)
    at_level = one_hot(levels, place_ref[1:2, :])
    contract = (((0,), (0,)), ((), ()))
    for which in range(2):
        for x in range(cells_x):
            wide_ref[...] = sum(x_ref[which, x, o] * row(x + o) for o in range(2 * HW + 1))
            held_ref[:, x * cells_y : (x + 1) * cells_y, :] = sum(
                y_ref[which, o][None] * wide_ref[:, o : o + cells_y, :] for o in range(2 * HW + 1)
            )
        top, low = halves(held_ref[...].reshape((members + 1) * cells, levels))
        z_top, z_low = halves(z_ref[which])
        smooth = (
            jnp.dot(top, z_top, preferred_element_type=F32)
            + jnp.dot(top, z_low, preferred_element_type=F32)
            + jnp.dot(low, z_top, preferred_element_type=F32)
        ).reshape(members + 1, cells, levels)
        static = (share * STATIC_WEIGHT) * sigma_ref[...] * smooth[members]
        parts = []
        for s in range(slots):
            part = sum(anomaly_ref[k, s].astype(F32) * smooth[k] for k in range(members))
            parts.append(ens_weight * part + static)
        field = jnp.concatenate(parts, axis=0)
        if which == 0:
            field_ref[...] = field
        top, low = halves(field)
        columns = lax.dot_general(
            top, at_cell, contract, preferred_element_type=F32
        ) + lax.dot_general(low, at_cell, contract, preferred_element_type=F32)
        value_ref[which : which + 1, :] = jnp.sum(
            jnp.where(at_level, columns, 0.0), axis=0, keepdims=True
        )


def mix_kernel(products_ref, first_ref, second_ref, total_ref, control_ref, static_ref, field_ref):
    sums = jnp.sum(jnp.sum(products_ref[...], axis=0), axis=1, keepdims=True)
    p00, p01, p11, p02, p12 = (sums[i : i + 1] for i in range(5))
    step0 = p00 / (p00 + p01)
    keep = 1.0 - step0
    next_norm = keep * (keep * p00 - 2.0 * step0 * p01) + step0 * step0 * p11
    beta = next_norm / p00
    lead = keep + beta
    own = lead * (lead * p00 - 2.0 * step0 * p01) + step0 * step0 * p11
    cross = lead * (lead * p01 - step0 * p02) - step0 * (lead * p11 - step0 * p12)
    step1 = next_norm / (own + cross)
    mix0 = step0 + step1 * lead
    mix1 = -step1 * step0
    members = control_ref.shape[0]
    for i in range(members):
        control_ref[i] = mix0 * first_ref[i] + mix1 * second_ref[i]
    static_ref[...] = mix0 * first_ref[members] + mix1 * second_ref[members]
    near = total_ref.shape[0]
    rows = field_ref.shape[0] // near
    skip = total_ref.shape[1] - 2 * rows
    for i in range(near):
        field_ref[i * rows : (i + 1) * rows, :] = (
            mix0 * total_ref[i, skip : skip + rows, :] + mix1 * total_ref[i, skip + rows :, :]
        )


def groups(size, width, stride):
    seen, out = set(), []
    for first in range(size):
        if first not in seen:
            members = [first + stride * k for k in range(width)]
            seen.update(members)
            out.append(members)
    return out


def exchange(blocks, axis, index_groups=None):
    return lax.all_to_all(blocks, axis, 0, 0, axis_index_groups=index_groups, tiled=True)


def gathered(block, width, axis, index_groups=None):
    return exchange(jnp.broadcast_to(block[None], (width,) + block.shape), axis, index_groups)


def neighbours(low_side, high_side, axis):
    count = lax.axis_size(axis)
    up = [(i, i + 1) for i in range(count - 1)]
    down = [(j, i) for i, j in up]
    return lax.ppermute(high_side, axis, up), lax.ppermute(low_side, axis, down)


def taps(field, table, dim, count):
    total = None
    for offset in range(2 * HW + 1):
        shape = [1] * field.ndim
        shape[dim] = count
        term = table[:, offset].reshape(shape) * lax.slice_in_dim(field, offset, offset + count, axis=dim)
        total = term if total is None else total + term
    return total


def flipped(table):
    rows = table.shape[0]
    padded = jnp.pad(table, ((HW, HW), (0, 0)))
    return jnp.stack([padded[o : o + rows, 2 * HW - o] for o in range(2 * HW + 1)], axis=1)


def window(table, axis, count, rim):
    padded = jnp.pad(table, ((rim, rim), (0, 0)))
    return lax.dynamic_slice_in_dim(padded, lax.axis_index(axis) * count, count + 2 * rim, 0)


def body(anomalies, sigma, taper_x, taper_y, taper_z, innovation, obs_inverse, obs_index, obs_slot):
    local_members, slots, cells_x, cells_y, levels = anomalies.shape
    member_devices = lax.axis_size("member")
    ens_weight = 0.8 / math.sqrt(local_members * member_devices - 1)
    share = 1.0 / member_devices
    cells = cells_x * cells_y
    count = obs_index.shape[-1]
    rows = count // levels

    near = 8 if member_devices % 8 == 0 else 1
    far = member_devices // near
    near_groups = groups(member_devices, near, 1)
    far_groups = groups(member_devices, far, near)
    close = 4 if member_devices % 4 == 0 else 1
    wide = member_devices // close
    close_groups = groups(member_devices, close, 1)
    wide_groups = groups(member_devices, wide, close)

    index_flat = obs_index.reshape(1, -1)
    place = jnp.concatenate(
        [obs_slot.reshape(1, -1) * cells + index_flat // levels, index_flat % levels], axis=0
    )
    obs_weight = obs_inverse.reshape(1, -1)
    first_weight = obs_weight * innovation.reshape(1, -1)

    x_rows = window(taper_x, "sx", cells_x, 0)
    x_flip = window(flipped(taper_x), "sx", cells_x, 0)
    y_rows_wide = window(taper_y, "sy", cells_y, HW)
    y_rows = y_rows_wide[HW : HW + cells_y]
    y_flip = window(flipped(taper_y), "sy", cells_y, 0)
    x_pair = jnp.stack([x_rows, x_flip])
    y_pair = jnp.broadcast_to(
        jnp.stack([y_rows.T, y_flip.T])[..., None], (2, 2 * HW + 1, cells_y, levels)
    )
    z_pair = jnp.stack([taper_z, taper_z.T])

    params = pltpu.CompilerParams(vmem_limit_bytes=40 * 2**20)
    packed = anomalies.reshape(local_members, slots, cells, levels)
    packed_sigma = sigma.reshape(cells, levels)
    side = cells_x * 2 * HW
    wide_y = cells_y + 2 * HW

    def apply(first, second):
        stack, low, high = pl.pallas_call(
            functools.partial(adjoint_kernel, ens_weight, cells_y),
            out_shape=(
                jax.ShapeDtypeStruct((local_members + 1, cells, levels), F32),
                jax.ShapeDtypeStruct((local_members + 1, side, levels), F32),
                jax.ShapeDtypeStruct((local_members + 1, side, levels), F32),
            ),
            compiler_params=params,
        )(place, first, second, packed, packed_sigma)
        left, right = neighbours(low, high, "sy")
        pieces = [
            block.reshape(local_members + 1, cells_x, -1, levels) for block in (left, stack, right)
        ]
        stack = taps(jnp.concatenate(pieces, axis=2), y_rows_wide, 2, wide_y)
        above, below = neighbours(stack[:, :HW], stack[:, cells_x - HW :], "sx")
        stack = taps(jnp.concatenate([above, stack, below], axis=1), x_rows, 1, cells_x)
        stack = jnp.einsum("bxyk,kl->bxyl", stack, taper_z, precision=HIGH)
        control = stack[:, :, HW : HW + cells_y]
        above, below = neighbours(stack[:, :HW], stack[:, cells_x - HW :], "sx")
        whole = pl.BlockSpec(memory_space=pltpu.VMEM)
        field, sampled = pl.pallas_call(
            functools.partial(forward_kernel, ens_weight, share),
            out_shape=(
                jax.ShapeDtypeStruct((slots * cells, levels), F32),
                jax.ShapeDtypeStruct((2, count), F32),
            ),
            in_specs=[pl.BlockSpec(memory_space=pltpu.SMEM)] + [whole] * 8,
            scratch_shapes=[
                pltpu.VMEM((local_members + 1, wide_y, levels), F32),
                pltpu.VMEM((local_members + 1, cells, levels), F32),
            ],
            compiler_params=params,
        )(x_pair, place, above, stack, below, y_pair, z_pair, packed, packed_sigma)
        return control, field, sampled.reshape(2, rows, levels)

    control0, field0, sampled0 = apply(obs_weight, innovation.reshape(1, -1))
    part = jnp.sum(gathered(sampled0[0], close, "member", close_groups), axis=0)
    seen0 = lax.psum(part, "member", axis_index_groups=wide_groups)
    obs_rows = obs_weight.reshape(rows, levels)
    weight1 = obs_rows * seen0
    control1, field1, sampled1 = apply(obs_weight, seen0.reshape(1, -1))

    flat = jnp.concatenate(
        [
            block.reshape(near, -1, levels)
            for block in (sampled0[1], sampled1[0], sampled1[1], field0, field1)
        ],
        axis=1,
    )
    chunk = jnp.sum(exchange(flat, "member", near_groups), axis=0)
    chunk = jnp.sum(gathered(chunk, far, "member", far_groups), axis=0)
    total = gathered(chunk, near, "member", near_groups)
    obs_chunk = rows // near
    seen = total[:, : 3 * obs_chunk].reshape(near, 3, obs_chunk, levels)
    flip0, seen1, flip1 = (seen[:, i].reshape(rows, levels) for i in range(3))

    weight0 = first_weight.reshape(rows, levels)
    weight2 = obs_rows * seen1
    products = jnp.stack(
        [
            jnp.sum(a * b, axis=0)
            for a, b in (
                (weight0, flip0),
                (weight1, flip0),
                (weight1, flip1),
                (weight2, flip0),
                (weight2, flip1),
            )
        ]
    )
    regions = lax.axis_size("sx") * lax.axis_size("sy")
    products = gathered(products, regions, ("sx", "sy"))
    control, static, increment = pl.pallas_call(
        mix_kernel,
        out_shape=(
            jax.ShapeDtypeStruct((local_members, cells, levels), F32),
            jax.ShapeDtypeStruct((cells, levels), F32),
            jax.ShapeDtypeStruct((slots * cells, levels), F32),
        ),
        compiler_params=params,
    )(
        products,
        control0.reshape(-1, cells, levels),
        control1.reshape(-1, cells, levels),
        total,
    )
    shape = (cells_x, cells_y, levels)
    return (
        control.reshape((local_members,) + shape),
        static.reshape(shape),
        increment.reshape((slots,) + shape),
    )


def solution(mesh):
    return jax.shard_map(
        body,
        mesh=mesh,
        in_specs=(
            P("member", None, "sx", "sy", None),
            P("sx", "sy", None),
            P(),
            P(),
            P(),
            P("sx", "sy", None),
            P("sx", "sy", None),
            P("sx", "sy", None),
            P("sx", "sy", None),
        ),
        out_specs=(P("member", "sx", "sy", None), P("sx", "sy", None), P(None, "sx", "sy", None)),
        check_vma=False,
    )
```

```python
import functools
import math

import jax
import jax.numpy as jnp
from jax import lax
from jax.experimental import pallas as pl
from jax.experimental.pallas import tpu as pltpu
from jax.sharding import PartitionSpec as P

HW = 3
STATIC_WEIGHT = 0.6
F32 = jnp.float32
BF16 = jnp.bfloat16
HIGH = lax.Precision.HIGH
HIGHEST = lax.Precision.HIGHEST


def halves(value):
    top = value.astype(BF16)
    return top, (value - top.astype(F32)).astype(BF16)


def one_hot(rows, index):
    return lax.broadcasted_iota(jnp.int32, (rows, index.shape[-1]), 0) == index


def observed(slot_ref, index_ref, slots, cells, levels):
    index = index_ref[...]
    column = lax.shift_right_logical(index, levels.bit_length() - 1)
    at_cell = one_hot(slots * cells, slot_ref[...] * cells + column).astype(BF16)
    return at_cell, one_hot(levels, index - column * levels)


def adjoint_kernel(
    ens_weight,
    cells_y,
    slot_ref,
    index_ref,
    first_ref,
    second_ref,
    anomaly_ref,
    sigma_ref,
    stack_ref,
    low_ref,
    high_ref,
):
    members, slots, cells, levels = anomaly_ref.shape
    at_cell, at_level = observed(slot_ref, index_ref, slots, cells, levels)
    top, low = halves(jnp.where(at_level, first_ref[...] * second_ref[...], 0.0))
    contract = (((1,), (1,)), ((), ()))
    grid = lax.dot_general(at_cell, top, contract, preferred_element_type=F32) + lax.dot_general(
        at_cell, low, contract, preferred_element_type=F32
    )
    parts = [grid[s * cells : (s + 1) * cells] for s in range(slots)]
    weighted = [ens_weight * part for part in parts]

    def put(k, field):
        stack_ref[k] = field
        for x in range(cells // cells_y):
            first, rim = x * cells_y, 2 * HW
            low_ref[k, x * rim : (x + 1) * rim, :] = field[first : first + rim]
            high_ref[k, x * rim : (x + 1) * rim, :] = field[first + cells_y - rim : first + cells_y]

    for k in range(members):
        put(k, sum(anomaly_ref[k, s].astype(F32) * weighted[s] for s in range(slots)))
    put(members, STATIC_WEIGHT * sigma_ref[...] * sum(parts))


def forward_kernel(
    ens_weight,
    share,
    x_ref,
    slot_ref,
    index_ref,
    stack_ref,
    y_ref,
    z_ref,
    anomaly_ref,
    sigma_ref,
    field_ref,
    value_ref,
    wide_ref,
    held_ref,
):
    members, slots, cells, levels = anomaly_ref.shape
    cells_x = x_ref.shape[1]
    cells_y = cells // cells_x
    at_cell, at_level = observed(slot_ref, index_ref, slots, cells, levels)
    contract = (((0,), (0,)), ((), ()))
    for which in range(2):
        for x in range(cells_x):
            wide_ref[...] = sum(x_ref[which, x, o] * stack_ref[:, x + o] for o in range(2 * HW + 1))
            held_ref[:, x * cells_y : (x + 1) * cells_y, :] = sum(
                y_ref[which, o][None] * wide_ref[:, o : o + cells_y, :] for o in range(2 * HW + 1)
            )
        top, low = halves(held_ref[...].reshape((members + 1) * cells, levels))
        z_top, z_low = halves(z_ref[which])
        smooth = (
            jnp.dot(top, z_top, preferred_element_type=F32)
            + jnp.dot(top, z_low, preferred_element_type=F32)
            + jnp.dot(low, z_top, preferred_element_type=F32)
        ).reshape(members + 1, cells, levels)
        static = (share * STATIC_WEIGHT) * sigma_ref[...] * smooth[members]
        parts = []
        for s in range(slots):
            part = sum(anomaly_ref[k, s].astype(F32) * smooth[k] for k in range(members))
            parts.append(ens_weight * part + static)
        field = jnp.concatenate(parts, axis=0)
        if which == 0:
            field_ref[...] = field
        top, low = halves(field)
        columns = lax.dot_general(
            top, at_cell, contract, preferred_element_type=F32
        ) + lax.dot_general(low, at_cell, contract, preferred_element_type=F32)
        value_ref[which : which + 1, :] = jnp.sum(
            jnp.where(at_level, columns, 0.0), axis=0, keepdims=True
        )


def product_kernel(total_ref, weight_ref, first_ref, seen_ref, products_ref):
    near = total_ref.shape[0]
    rows, levels = weight_ref.shape
    part = rows // near

    def sampled(which):
        pieces = [total_ref[i, which * part : (which + 1) * part, :] for i in range(near)]
        return jnp.concatenate(pieces, axis=0)

    flip0, seen1, flip1 = (sampled(which) for which in range(3))
    weight0 = weight_ref[...] * first_ref[...]
    weight1 = weight_ref[...] * seen_ref[...]
    weight2 = weight_ref[...] * seen1
    pairs = (
        (weight0, flip0),
        (weight1, flip0),
        (weight1, flip1),
        (weight2, flip0),
        (weight2, flip1),
    )
    sums = [jnp.sum(a * b, axis=0, keepdims=True) for a, b in pairs]
    sums.append(jnp.zeros((products_ref.shape[1] - len(pairs), levels), F32))
    products_ref[...] = jnp.broadcast_to(jnp.concatenate(sums, axis=0)[None], products_ref.shape)


def mix_kernel(products_ref, first_ref, second_ref, total_ref, control_ref, static_ref, field_ref):
    sums = jnp.sum(jnp.sum(products_ref[...], axis=0), axis=1, keepdims=True)
    p00, p01, p11, p02, p12 = (sums[i : i + 1] for i in range(5))
    step0 = p00 / (p00 + p01)
    keep = 1.0 - step0
    next_norm = keep * (keep * p00 - 2.0 * step0 * p01) + step0 * step0 * p11
    beta = next_norm / p00
    lead = keep + beta
    own = lead * (lead * p00 - 2.0 * step0 * p01) + step0 * step0 * p11
    cross = lead * (lead * p01 - step0 * p02) - step0 * (lead * p11 - step0 * p12)
    step1 = next_norm / (own + cross)
    mix0 = step0 + step1 * lead
    mix1 = -step1 * step0
    members = control_ref.shape[0]
    for i in range(members):
        control_ref[i] = mix0 * first_ref[i] + mix1 * second_ref[i]
    static_ref[...] = mix0 * first_ref[members] + mix1 * second_ref[members]
    near = total_ref.shape[0]
    rows = field_ref.shape[0] // near
    skip = total_ref.shape[1] - 2 * rows
    for i in range(near):
        field_ref[i * rows : (i + 1) * rows, :] = (
            mix0 * total_ref[i, skip : skip + rows, :] + mix1 * total_ref[i, skip + rows :, :]
        )


def groups(size, width, stride):
    seen, out = set(), []
    for first in range(size):
        if first not in seen:
            members = [first + stride * k for k in range(width)]
            seen.update(members)
            out.append(members)
    return out


def exchange(blocks, axis, index_groups=None):
    return lax.all_to_all(blocks, axis, 0, 0, axis_index_groups=index_groups, tiled=True)


def gathered(block, width, axis, index_groups=None):
    return exchange(jnp.broadcast_to(block[None], (width,) + block.shape), axis, index_groups)


def neighbours(low_side, high_side, axis):
    count = lax.axis_size(axis)
    up = [(i, i + 1) for i in range(count - 1)]
    down = [(j, i) for i, j in up]
    return lax.ppermute(high_side, axis, up), lax.ppermute(low_side, axis, down)


def paired(low_side, high_side, axis):
    count = lax.axis_size(axis)
    place = lax.axis_index(axis)
    even = [(i, i + 1) for i in range(0, count - 1, 2)]
    odd = [(i, i + 1) for i in range(1, count - 1, 2)]
    upper = lax.rem(place, 2) == 1
    far = lax.ppermute(jnp.where(upper, high_side, low_side), axis, odd + [(j, i) for i, j in odd])
    close = lax.ppermute(jnp.where(upper, low_side, high_side), axis, even + [(j, i) for i, j in even])
    return jnp.where(upper, close, far), jnp.where(upper, far, close)


def widened(block, extra, axis):
    size = block.shape[1]
    place = lax.axis_index(axis)
    upper = place >= 2
    edge = jnp.where(upper, block[:, :extra], block[:, size - extra :])
    beyond = lax.ppermute(edge, axis, [(0, 2), (2, 0), (1, 3), (3, 1)])
    above, below = paired(block, block, axis)
    none = jnp.zeros_like(beyond)
    return jnp.concatenate(
        [jnp.where(upper, beyond, none), above, block, below, jnp.where(upper, none, beyond)], axis=1
    )


def taps(field, table, dim, count):
    total = None
    for offset in range(2 * HW + 1):
        shape = [1] * field.ndim
        shape[dim] = count
        term = table[:, offset].reshape(shape) * lax.slice_in_dim(field, offset, offset + count, axis=dim)
        total = term if total is None else total + term
    return total


def flipped(table):
    rows = table.shape[0]
    padded = jnp.pad(table, ((HW, HW), (0, 0)))
    return jnp.stack([padded[o : o + rows, 2 * HW - o] for o in range(2 * HW + 1)], axis=1)


def window(table, axis, count, rim):
    padded = jnp.pad(table, ((rim, rim), (0, 0)))
    return lax.dynamic_slice_in_dim(padded, lax.axis_index(axis) * count, count + 2 * rim, 0)


def body(anomalies, sigma, taper_x, taper_y, taper_z, innovation, obs_inverse, obs_index, obs_slot):
    local_members, slots, cells_x, cells_y, levels = anomalies.shape
    member_devices = lax.axis_size("member")
    ens_weight = 0.8 / math.sqrt(local_members * member_devices - 1)
    share = 1.0 / member_devices
    cells = cells_x * cells_y
    count = obs_index.shape[-1]
    rows = count // levels

    near = 8 if member_devices % 8 == 0 else 1
    far = member_devices // near
    near_groups = groups(member_devices, near, 1)
    far_groups = groups(member_devices, far, near)
    close = 4 if member_devices % 4 == 0 else 1
    wide = member_devices // close
    close_groups = groups(member_devices, close, 1)
    wide_groups = groups(member_devices, wide, close)

    index = obs_index.reshape(1, -1)
    slot = obs_slot.reshape(1, -1)
    obs_weight = obs_inverse.reshape(1, -1)
    first = innovation.reshape(1, -1)

    x_rows_wide = window(taper_x, "sx", cells_x, HW)
    x_rows = x_rows_wide[HW : HW + cells_x]
    x_flip = window(flipped(taper_x), "sx", cells_x, 0)
    y_rows_wide = window(taper_y, "sy", cells_y, HW)
    y_rows = y_rows_wide[HW : HW + cells_y]
    y_flip = window(flipped(taper_y), "sy", cells_y, 0)
    x_pair = jnp.stack([x_rows, x_flip])
    y_pair = jnp.broadcast_to(
        jnp.stack([y_rows.T, y_flip.T])[..., None], (2, 2 * HW + 1, cells_y, levels)
    )
    z_pair = jnp.stack([taper_z, taper_z.T])

    params = pltpu.CompilerParams(vmem_limit_bytes=40 * 2**20)
    packed = anomalies.reshape(local_members, slots, cells, levels)
    packed_sigma = sigma.reshape(cells, levels)
    side = cells_x * 2 * HW
    wide_y = cells_y + 2 * HW

    def apply(first, second, room):
        stack, low, high = pl.pallas_call(
            functools.partial(adjoint_kernel, ens_weight, cells_y),
            out_shape=(
                jax.ShapeDtypeStruct((local_members + 1, cells, levels), F32),
                jax.ShapeDtypeStruct((local_members + 1, side, levels), F32),
                jax.ShapeDtypeStruct((local_members + 1, side, levels), F32),
            ),
            compiler_params=pltpu.CompilerParams(vmem_limit_bytes=room * 2**20),
        )(slot, index, first, second, packed, packed_sigma)
        left, right = neighbours(low, high, "sy")
        pieces = [
            block.reshape(local_members + 1, cells_x, -1, levels) for block in (left, stack, right)
        ]
        stack = taps(jnp.concatenate(pieces, axis=2), y_rows_wide, 2, wide_y)
        stack = taps(widened(stack, 2 * HW - cells_x, "sx"), x_rows_wide, 1, cells_x + 2 * HW)
        stack = jnp.einsum("bxyk,kl->bxyl", stack, taper_z, precision=HIGH)
        control = stack[:, HW : HW + cells_x, HW : HW + cells_y]
        whole = pl.BlockSpec(memory_space=pltpu.VMEM)
        field, sampled = pl.pallas_call(
            functools.partial(forward_kernel, ens_weight, share),
            out_shape=(
                jax.ShapeDtypeStruct((slots * cells, levels), F32),
                jax.ShapeDtypeStruct((2, count), F32),
            ),
            in_specs=[pl.BlockSpec(memory_space=pltpu.SMEM)] + [whole] * 7,
            scratch_shapes=[
                pltpu.VMEM((local_members + 1, wide_y, levels), F32),
                pltpu.VMEM((local_members + 1, cells, levels), F32),
            ],
            compiler_params=params,
        )(x_pair, slot, index, stack, y_pair, z_pair, packed, packed_sigma)
        return control, field, sampled.reshape(2, rows, levels)

    control0, field0, sampled0 = apply(obs_weight, first, 60)
    part = jnp.sum(gathered(sampled0[0], close, "member", close_groups), axis=0)
    seen0 = lax.psum(part, "member", axis_index_groups=wide_groups)
    control1, field1, sampled1 = apply(obs_weight, seen0.reshape(1, -1), 40)

    blocks = (sampled0[1], sampled1[0], sampled1[1], field0, field1)
    flat = jnp.concatenate([block.reshape(near, -1, levels) for block in blocks], axis=1)
    chunk = jnp.sum(exchange(flat, "member", near_groups), axis=0)
    chunk = jnp.sum(gathered(chunk, far, "member", far_groups), axis=0)
    total = gathered(chunk, near, "member", near_groups)
    regions = lax.axis_size("sx") * lax.axis_size("sy")
    products = pl.pallas_call(
        product_kernel,
        out_shape=jax.ShapeDtypeStruct((regions, 8, levels), F32),
        compiler_params=params,
    )(total, obs_inverse.reshape(rows, levels), innovation.reshape(rows, levels), seen0)
    products = exchange(products, ("sx", "sy"))
    control, static, increment = pl.pallas_call(
        mix_kernel,
        out_shape=(
            jax.ShapeDtypeStruct((local_members, cells, levels), F32),
            jax.ShapeDtypeStruct((cells, levels), F32),
            jax.ShapeDtypeStruct((slots * cells, levels), F32),
        ),
        compiler_params=params,
    )(
        products,
        control0.reshape(-1, cells, levels),
        control1.reshape(-1, cells, levels),
        total,
    )
    shape = (cells_x, cells_y, levels)
    return (
        control.reshape((local_members,) + shape),
        static.reshape(shape),
        increment.reshape((slots,) + shape),
    )


def solution(mesh):
    return jax.shard_map(
        body,
        mesh=mesh,
        in_specs=(
            P("member", None, "sx", "sy", None),
            P("sx", "sy", None),
            P(),
            P(),
            P(),
            P("sx", "sy", None),
            P("sx", "sy", None),
            P("sx", "sy", None),
            P("sx", "sy", None),
        ),
        out_specs=(P("member", "sx", "sy", None), P("sx", "sy", None), P(None, "sx", "sy", None)),
        check_vma=False,
    )
```

```python
import functools
import math

import jax
import jax.numpy as jnp
from jax import lax
from jax.experimental import pallas as pl
from jax.experimental.pallas import tpu as pltpu
from jax.sharding import PartitionSpec as P

HW = 3
STATIC_WEIGHT = 0.6
F32 = jnp.float32
BF16 = jnp.bfloat16
HIGHEST = lax.Precision.HIGHEST


def halves(value):
    top = value.astype(BF16)
    return top, (value - top.astype(F32)).astype(BF16)


def product(value, weights):
    top, low = halves(value)
    w_top, w_low = halves(weights)
    pair = jnp.concatenate(
        [
            jnp.concatenate([w_top, w_low], axis=1),
            jnp.concatenate([w_top, jnp.zeros_like(w_low)], axis=1),
        ],
        axis=0,
    )
    both = jnp.dot(jnp.concatenate([top, low], axis=1), pair, preferred_element_type=F32)
    return both[:, : weights.shape[1]] + both[:, weights.shape[1] :]


def one_hot(rows, index):
    return lax.broadcasted_iota(jnp.int32, (rows, index.shape[-1]), 0) == index


def observed(slot_ref, index_ref, slots, cells, levels):
    index = index_ref[...]
    column = lax.shift_right_logical(index, levels.bit_length() - 1)
    at_cell = one_hot(slots * cells, slot_ref[...] * cells + column).astype(BF16)
    return at_cell, one_hot(levels, index - column * levels)


def adjoint_kernel(
    ens_weight,
    cells_y,
    slot_ref,
    index_ref,
    first_ref,
    second_ref,
    anomaly_ref,
    sigma_ref,
    stack_ref,
    low_ref,
    high_ref,
):
    members, slots, cells, levels = anomaly_ref.shape
    at_cell, at_level = observed(slot_ref, index_ref, slots, cells, levels)
    top, low = halves(jnp.where(at_level, first_ref[...] * second_ref[...], 0.0))
    both = lax.dot_general(
        at_cell,
        jnp.concatenate([top, low], axis=0),
        (((1,), (1,)), ((), ())),
        preferred_element_type=F32,
    )
    grid = both[:, :levels] + both[:, levels:]
    parts = [grid[s * cells : (s + 1) * cells] for s in range(slots)]
    weighted = [ens_weight * part for part in parts]

    def put(k, field):
        stack_ref[k] = field
        for x in range(cells // cells_y):
            first, rim = x * cells_y, 2 * HW
            low_ref[k, x * rim : (x + 1) * rim, :] = field[first : first + rim]
            high_ref[k, x * rim : (x + 1) * rim, :] = field[first + cells_y - rim : first + cells_y]

    for k in range(members):
        put(k, sum(anomaly_ref[k, s].astype(F32) * weighted[s] for s in range(slots)))
    put(members, STATIC_WEIGHT * sigma_ref[...] * sum(parts))


def forward_kernel(
    ens_weight,
    share,
    x_ref,
    slot_ref,
    index_ref,
    stack_ref,
    y_ref,
    z_ref,
    anomaly_ref,
    sigma_ref,
    field_ref,
    value_ref,
    wide_ref,
    held_ref,
):
    members, slots, cells, levels = anomaly_ref.shape
    cells_x = x_ref.shape[1]
    cells_y = cells // cells_x
    at_cell, at_level = observed(slot_ref, index_ref, slots, cells, levels)
    pieces = []
    for which in range(2):
        for x in range(cells_x):
            wide_ref[...] = sum(x_ref[which, x, o] * stack_ref[:, x + o] for o in range(2 * HW + 1))
            held_ref[:, x * cells_y : (x + 1) * cells_y, :] = sum(
                y_ref[which, o][None] * wide_ref[:, o : o + cells_y, :] for o in range(2 * HW + 1)
            )
        flat = held_ref[...].reshape((members + 1) * cells, levels)
        smooth = product(flat, z_ref[which]).reshape(members + 1, cells, levels)
        static = (share * STATIC_WEIGHT) * sigma_ref[...] * smooth[members]
        parts = []
        for s in range(slots):
            part = sum(anomaly_ref[k, s].astype(F32) * smooth[k] for k in range(members))
            parts.append(ens_weight * part + static)
        field = jnp.concatenate(parts, axis=0)
        if which == 0:
            field_ref[...] = field
        pieces.extend(halves(field))
    columns = lax.dot_general(
        jnp.concatenate(pieces, axis=1),
        at_cell,
        (((0,), (0,)), ((), ())),
        preferred_element_type=F32,
    )
    for which in range(2):
        first = 2 * which * levels
        column = columns[first : first + levels] + columns[first + levels : first + 2 * levels]
        value_ref[which : which + 1, :] = jnp.sum(
            jnp.where(at_level, column, 0.0), axis=0, keepdims=True
        )


def product_kernel(total_ref, weight_ref, first_ref, seen_ref, products_ref):
    near = total_ref.shape[0]
    rows, levels = weight_ref.shape
    part = rows // near

    def sampled(which):
        pieces = [total_ref[i, which * part : (which + 1) * part, :] for i in range(near)]
        return jnp.concatenate(pieces, axis=0)

    flip0, seen1, flip1 = (sampled(which) for which in range(3))
    weight0 = weight_ref[...] * first_ref[...]
    weight1 = weight_ref[...] * seen_ref[...]
    weight2 = weight_ref[...] * seen1
    pairs = (
        (weight0, flip0),
        (weight1, flip0),
        (weight1, flip1),
        (weight2, flip0),
        (weight2, flip1),
    )
    sums = [jnp.sum(a * b, axis=0, keepdims=True) for a, b in pairs]
    sums.append(jnp.zeros((products_ref.shape[1] - len(pairs), levels), F32))
    products_ref[...] = jnp.broadcast_to(jnp.concatenate(sums, axis=0)[None], products_ref.shape)


def mix_kernel(
    products_ref, first_ref, second_ref, z_ref, total_ref, control_ref, static_ref, field_ref
):
    sums = jnp.sum(jnp.sum(products_ref[...], axis=0), axis=1, keepdims=True)
    p00, p01, p11, p02, p12 = (sums[i : i + 1] for i in range(5))
    step0 = p00 / (p00 + p01)
    keep = 1.0 - step0
    next_norm = keep * (keep * p00 - 2.0 * step0 * p01) + step0 * step0 * p11
    beta = next_norm / p00
    lead = keep + beta
    own = lead * (lead * p00 - 2.0 * step0 * p01) + step0 * step0 * p11
    cross = lead * (lead * p01 - step0 * p02) - step0 * (lead * p11 - step0 * p12)
    step1 = next_norm / (own + cross)
    mix0 = step0 + step1 * lead
    mix1 = -step1 * step0
    members, cells, levels = control_ref.shape
    mixed = (mix0 * first_ref[...] + mix1 * second_ref[...]).reshape(-1, levels)
    smooth = product(mixed, z_ref[...])
    control_ref[...] = smooth[: members * cells].reshape(members, cells, levels)
    static_ref[...] = smooth[members * cells :]
    near = total_ref.shape[0]
    rows = field_ref.shape[0] // near
    skip = total_ref.shape[1] - 2 * rows
    for i in range(near):
        field_ref[i * rows : (i + 1) * rows, :] = (
            mix0 * total_ref[i, skip : skip + rows, :] + mix1 * total_ref[i, skip + rows :, :]
        )


def groups(size, width, stride):
    seen, out = set(), []
    for first in range(size):
        if first not in seen:
            members = [first + stride * k for k in range(width)]
            seen.update(members)
            out.append(members)
    return out


def exchange(blocks, axis, index_groups=None):
    return lax.all_to_all(blocks, axis, 0, 0, axis_index_groups=index_groups, tiled=True)


def gathered(block, width, axis, index_groups=None):
    return exchange(jnp.broadcast_to(block[None], (width,) + block.shape), axis, index_groups)


def neighbours(low_side, high_side, axis):
    count = lax.axis_size(axis)
    up = [(i, i + 1) for i in range(count - 1)]
    down = [(j, i) for i, j in up]
    return lax.ppermute(high_side, axis, up), lax.ppermute(low_side, axis, down)


def paired(low_side, high_side, axis):
    count = lax.axis_size(axis)
    place = lax.axis_index(axis)
    even = [(i, i + 1) for i in range(0, count - 1, 2)]
    odd = [(i, i + 1) for i in range(1, count - 1, 2)]
    upper = lax.rem(place, 2) == 1
    far = lax.ppermute(jnp.where(upper, high_side, low_side), axis, odd + [(j, i) for i, j in odd])
    close = lax.ppermute(jnp.where(upper, low_side, high_side), axis, even + [(j, i) for i, j in even])
    return jnp.where(upper, close, far), jnp.where(upper, far, close)


def widened(block, extra, axis):
    size = block.shape[1]
    place = lax.axis_index(axis)
    upper = place >= 2
    edge = jnp.where(upper, block[:, :extra], block[:, size - extra :])
    beyond = lax.ppermute(edge, axis, [(0, 2), (2, 0), (1, 3), (3, 1)])
    above, below = paired(block, block, axis)
    none = jnp.zeros_like(beyond)
    return jnp.concatenate(
        [jnp.where(upper, beyond, none), above, block, below, jnp.where(upper, none, beyond)], axis=1
    )


def taps(field, table, dim, count):
    total = None
    for offset in range(2 * HW + 1):
        shape = [1] * field.ndim
        shape[dim] = count
        term = table[:, offset].reshape(shape) * lax.slice_in_dim(field, offset, offset + count, axis=dim)
        total = term if total is None else total + term
    return total


def flipped(wide, count):
    return jnp.stack([wide[o : o + count, 2 * HW - o] for o in range(2 * HW + 1)], axis=1)


def window(table, axis, count, rim):
    padded = jnp.pad(table, ((rim, rim), (0, 0)))
    return lax.dynamic_slice_in_dim(padded, lax.axis_index(axis) * count, count + 2 * rim, 0)


def body(anomalies, sigma, taper_x, taper_y, taper_z, innovation, obs_inverse, obs_index, obs_slot):
    local_members, slots, cells_x, cells_y, levels = anomalies.shape
    member_devices = lax.axis_size("member")
    ens_weight = 0.8 / math.sqrt(local_members * member_devices - 1)
    share = 1.0 / member_devices
    cells = cells_x * cells_y
    count = obs_index.shape[-1]
    rows = count // levels

    near = 4 if member_devices % 4 == 0 else 1
    far = member_devices // near
    near_groups = groups(member_devices, near, 1)
    far_groups = groups(member_devices, far, near)

    index = obs_index.reshape(1, -1)
    slot = obs_slot.reshape(1, -1)
    obs_weight = obs_inverse.reshape(1, -1)
    first = innovation.reshape(1, -1)

    x_rows_wide = window(taper_x, "sx", cells_x, HW)
    x_rows = x_rows_wide[HW : HW + cells_x]
    x_flip = flipped(x_rows_wide, cells_x)
    y_rows_wide = window(taper_y, "sy", cells_y, HW)
    y_rows = y_rows_wide[HW : HW + cells_y]
    y_flip = flipped(y_rows_wide, cells_y)
    x_pair = jnp.stack([x_rows, x_flip])
    y_pair = jnp.broadcast_to(
        jnp.stack([y_rows.T, y_flip.T])[..., None], (2, 2 * HW + 1, cells_y, levels)
    )

    params = pltpu.CompilerParams(vmem_limit_bytes=40 * 2**20)
    packed = anomalies.reshape(local_members, slots, cells, levels)
    packed_sigma = sigma.reshape(cells, levels)
    side = cells_x * 2 * HW
    wide_y = cells_y + 2 * HW

    whole = pl.BlockSpec(memory_space=pltpu.VMEM)

    def z_products(after):
        table, after = lax.optimization_barrier((taper_z, after))
        return jnp.stack(
            [jnp.dot(table, other, precision=HIGHEST) for other in (table, table.T)]
        ), after

    def apply(first, second, room, z_pair=None):
        stack, low, high = pl.pallas_call(
            functools.partial(adjoint_kernel, ens_weight, cells_y),
            out_shape=(
                jax.ShapeDtypeStruct((local_members + 1, cells, levels), F32),
                jax.ShapeDtypeStruct((local_members + 1, side, levels), F32),
                jax.ShapeDtypeStruct((local_members + 1, side, levels), F32),
            ),
            compiler_params=pltpu.CompilerParams(vmem_limit_bytes=room * 2**20),
        )(slot, index, first, second, packed, packed_sigma)
        left, right = neighbours(low, high, "sy")
        pieces = [
            block.reshape(local_members + 1, cells_x, -1, levels) for block in (left, stack, right)
        ]
        stack = taps(jnp.concatenate(pieces, axis=2), y_rows_wide, 2, wide_y)
        if z_pair is None:
            z_pair, stack = z_products(stack)
        stack = taps(widened(stack, 2 * HW - cells_x, "sx"), x_rows_wide, 1, cells_x + 2 * HW)
        control = stack[:, HW : HW + cells_x, HW : HW + cells_y]
        field, sampled = pl.pallas_call(
            functools.partial(forward_kernel, ens_weight, share),
            out_shape=(
                jax.ShapeDtypeStruct((slots * cells, levels), F32),
                jax.ShapeDtypeStruct((2, count), F32),
            ),
            in_specs=[pl.BlockSpec(memory_space=pltpu.SMEM)] + [whole] * 7,
            scratch_shapes=[
                pltpu.VMEM((local_members + 1, wide_y, levels), F32),
                pltpu.VMEM((local_members + 1, cells, levels), F32),
            ],
            compiler_params=params,
        )(x_pair, slot, index, stack, y_pair, z_pair, packed, packed_sigma)
        return control, field, sampled.reshape(2, rows, levels), z_pair

    control0, field0, sampled0, z_pair = apply(obs_weight, first, 60)
    part = jnp.sum(gathered(sampled0[0], near, "member", near_groups), axis=0)
    seen0 = lax.psum(part, "member", axis_index_groups=far_groups)
    control1, field1, sampled1, _ = apply(obs_weight, seen0.reshape(1, -1), 40, z_pair)

    blocks = (sampled0[1], sampled1[0], sampled1[1], field0, field1)
    flat = jnp.concatenate([block.reshape(near, -1, levels) for block in blocks], axis=1)
    chunk = jnp.sum(exchange(flat, "member", near_groups), axis=0)
    chunk = lax.psum(chunk, "member", axis_index_groups=far_groups)
    total = gathered(chunk, near, "member", near_groups)
    regions = lax.axis_size("sx") * lax.axis_size("sy")
    products = pl.pallas_call(
        product_kernel,
        out_shape=jax.ShapeDtypeStruct((regions, 8, levels), F32),
        compiler_params=params,
    )(total, obs_inverse.reshape(rows, levels), innovation.reshape(rows, levels), seen0)
    products = exchange(products, ("sx", "sy"))
    control, static, increment = pl.pallas_call(
        mix_kernel,
        out_shape=(
            jax.ShapeDtypeStruct((local_members, cells, levels), F32),
            jax.ShapeDtypeStruct((cells, levels), F32),
            jax.ShapeDtypeStruct((slots * cells, levels), F32),
        ),
        compiler_params=params,
    )(
        products,
        control0.reshape(-1, cells, levels),
        control1.reshape(-1, cells, levels),
        taper_z,
        total,
    )
    shape = (cells_x, cells_y, levels)
    return (
        control.reshape((local_members,) + shape),
        static.reshape(shape),
        increment.reshape((slots,) + shape),
    )


def solution(mesh):
    return jax.shard_map(
        body,
        mesh=mesh,
        in_specs=(
            P("member", None, "sx", "sy", None),
            P("sx", "sy", None),
            P(),
            P(),
            P(),
            P("sx", "sy", None),
            P("sx", "sy", None),
            P("sx", "sy", None),
            P("sx", "sy", None),
        ),
        out_specs=(P("member", "sx", "sy", None), P("sx", "sy", None), P(None, "sx", "sy", None)),
        check_vma=False,
    )
```

```python
import functools
import math

import jax
import jax.numpy as jnp
from jax import lax
from jax.experimental import pallas as pl
from jax.experimental.pallas import tpu as pltpu
from jax.sharding import PartitionSpec as P

HW = 3
STATIC_WEIGHT = 0.6
F32 = jnp.float32
BF16 = jnp.bfloat16
HIGHEST = lax.Precision.HIGHEST


def halves(value):
    top = value.astype(BF16)
    return top, (value - top.astype(F32)).astype(BF16)


def product(value, weights):
    top, low = halves(value)
    w_top, w_low = halves(weights)
    pair = jnp.concatenate(
        [
            jnp.concatenate([w_top, w_low], axis=1),
            jnp.concatenate([w_top, jnp.zeros_like(w_low)], axis=1),
        ],
        axis=0,
    )
    both = jnp.dot(jnp.concatenate([top, low], axis=1), pair, preferred_element_type=F32)
    return both[:, : weights.shape[1]] + both[:, weights.shape[1] :]


def one_hot(rows, index):
    return lax.broadcasted_iota(jnp.int32, (rows, index.shape[-1]), 0) == index


def observed(slot_ref, index_ref, slots, cells, levels):
    index = index_ref[...]
    column = lax.shift_right_logical(index, levels.bit_length() - 1)
    at_cell = one_hot(slots * cells, slot_ref[...] * cells + column).astype(BF16)
    return at_cell, one_hot(levels, index - column * levels)


def adjoint_kernel(
    ens_weight,
    cells_y,
    slot_ref,
    index_ref,
    first_ref,
    second_ref,
    anomaly_ref,
    sigma_ref,
    stack_ref,
    low_ref,
    high_ref,
):
    members, slots, cells, levels = anomaly_ref.shape
    at_cell, at_level = observed(slot_ref, index_ref, slots, cells, levels)
    top, low = halves(jnp.where(at_level, first_ref[...] * second_ref[...], 0.0))
    both = lax.dot_general(
        at_cell,
        jnp.concatenate([top, low], axis=0),
        (((1,), (1,)), ((), ())),
        preferred_element_type=F32,
    )
    grid = both[:, :levels] + both[:, levels:]
    parts = [grid[s * cells : (s + 1) * cells] for s in range(slots)]
    weighted = [ens_weight * part for part in parts]

    def put(k, field):
        stack_ref[k] = field
        for x in range(cells // cells_y):
            first, rim = x * cells_y, 2 * HW
            low_ref[k, x * rim : (x + 1) * rim, :] = field[first : first + rim]
            high_ref[k, x * rim : (x + 1) * rim, :] = field[first + cells_y - rim : first + cells_y]

    for k in range(members):
        put(k, sum(anomaly_ref[k, s].astype(F32) * weighted[s] for s in range(slots)))
    put(members, STATIC_WEIGHT * sigma_ref[...] * sum(parts))


def forward_kernel(
    ens_weight,
    share,
    x_ref,
    slot_ref,
    index_ref,
    stack_ref,
    y_ref,
    z_ref,
    anomaly_ref,
    sigma_ref,
    field_ref,
    value_ref,
    wide_ref,
    held_ref,
):
    members, slots, cells, levels = anomaly_ref.shape
    cells_x = x_ref.shape[1]
    cells_y = cells // cells_x
    at_cell, at_level = observed(slot_ref, index_ref, slots, cells, levels)
    pieces = []
    for which in range(2):
        for x in range(cells_x):
            wide_ref[...] = sum(x_ref[which, x, o] * stack_ref[:, x + o] for o in range(2 * HW + 1))
            held_ref[:, x * cells_y : (x + 1) * cells_y, :] = sum(
                y_ref[which, o][None] * wide_ref[:, o : o + cells_y, :] for o in range(2 * HW + 1)
            )
        flat = held_ref[...].reshape((members + 1) * cells, levels)
        smooth = product(flat, z_ref[which]).reshape(members + 1, cells, levels)
        static = (share * STATIC_WEIGHT) * sigma_ref[...] * smooth[members]
        parts = []
        for s in range(slots):
            part = sum(anomaly_ref[k, s].astype(F32) * smooth[k] for k in range(members))
            parts.append(ens_weight * part + static)
        field = jnp.concatenate(parts, axis=0)
        if which == 0:
            field_ref[...] = field
        pieces.extend(halves(field))
    columns = lax.dot_general(
        jnp.concatenate(pieces, axis=1),
        at_cell,
        (((0,), (0,)), ((), ())),
        preferred_element_type=F32,
    )
    for which in range(2):
        first = 2 * which * levels
        column = columns[first : first + levels] + columns[first + levels : first + 2 * levels]
        value_ref[which : which + 1, :] = jnp.sum(
            jnp.where(at_level, column, 0.0), axis=0, keepdims=True
        )


def product_kernel(total_ref, weight_ref, first_ref, seen_ref, products_ref):
    near = total_ref.shape[0]
    rows, levels = weight_ref.shape
    part = rows // near

    def sampled(which):
        pieces = [total_ref[i, which * part : (which + 1) * part, :] for i in range(near)]
        return jnp.concatenate(pieces, axis=0)

    flip0, seen1, flip1 = (sampled(which) for which in range(3))
    weight0 = weight_ref[...] * first_ref[...]
    weight1 = weight_ref[...] * seen_ref[...]
    weight2 = weight_ref[...] * seen1
    pairs = (
        (weight0, flip0),
        (weight1, flip0),
        (weight1, flip1),
        (weight2, flip0),
        (weight2, flip1),
    )
    lane = lax.broadcasted_iota(jnp.int32, (1, levels), 1)
    line = jnp.zeros((1, levels), F32)
    for i, (a, b) in enumerate(pairs):
        column = jnp.sum(a * b, axis=0, keepdims=True)
        line = jnp.where(lane == i, jnp.sum(column, axis=1, keepdims=True), line)
    products_ref[...] = jnp.broadcast_to(line, products_ref.shape)


def mix_kernel(
    products_ref, first_ref, second_ref, z_ref, total_ref, control_ref, static_ref, field_ref
):
    sums = jnp.sum(products_ref[...], axis=0, keepdims=True)
    p00, p01, p11, p02, p12 = (sums[:, i : i + 1] for i in range(5))
    step0 = p00 / (p00 + p01)
    keep = 1.0 - step0
    next_norm = keep * (keep * p00 - 2.0 * step0 * p01) + step0 * step0 * p11
    beta = next_norm / p00
    lead = keep + beta
    own = lead * (lead * p00 - 2.0 * step0 * p01) + step0 * step0 * p11
    cross = lead * (lead * p01 - step0 * p02) - step0 * (lead * p11 - step0 * p12)
    step1 = next_norm / (own + cross)
    mix0 = step0 + step1 * lead
    mix1 = -step1 * step0
    members, cells, levels = control_ref.shape
    mixed = (mix0 * first_ref[...] + mix1 * second_ref[...]).reshape(-1, levels)
    smooth = product(mixed, z_ref[...])
    control_ref[...] = smooth[: members * cells].reshape(members, cells, levels)
    static_ref[...] = smooth[members * cells :]
    near = total_ref.shape[0]
    rows = field_ref.shape[0] // near
    skip = total_ref.shape[1] - 2 * rows
    for i in range(near):
        field_ref[i * rows : (i + 1) * rows, :] = (
            mix0 * total_ref[i, skip : skip + rows, :] + mix1 * total_ref[i, skip + rows :, :]
        )


def groups(size, width, stride):
    seen, out = set(), []
    for first in range(size):
        if first not in seen:
            members = [first + stride * k for k in range(width)]
            seen.update(members)
            out.append(members)
    return out


def exchange(blocks, axis, index_groups=None):
    return lax.all_to_all(blocks, axis, 0, 0, axis_index_groups=index_groups, tiled=True)


def gathered(block, width, axis, index_groups=None):
    return exchange(jnp.broadcast_to(block[None], (width,) + block.shape), axis, index_groups)


def neighbours(low_side, high_side, axis):
    count = lax.axis_size(axis)
    up = [(i, i + 1) for i in range(count - 1)]
    down = [(j, i) for i, j in up]
    return lax.ppermute(high_side, axis, up), lax.ppermute(low_side, axis, down)


def paired(low_side, high_side, axis):
    count = lax.axis_size(axis)
    place = lax.axis_index(axis)
    even = [(i, i + 1) for i in range(0, count - 1, 2)]
    odd = [(i, i + 1) for i in range(1, count - 1, 2)]
    upper = lax.rem(place, 2) == 1
    far = lax.ppermute(jnp.where(upper, high_side, low_side), axis, odd + [(j, i) for i, j in odd])
    close = lax.ppermute(jnp.where(upper, low_side, high_side), axis, even + [(j, i) for i, j in even])
    return jnp.where(upper, close, far), jnp.where(upper, far, close)


def widened(block, extra, axis):
    size = block.shape[1]
    place = lax.axis_index(axis)
    upper = place >= 2
    edge = jnp.where(upper, block[:, :extra], block[:, size - extra :])
    beyond = lax.ppermute(edge, axis, [(0, 2), (2, 0), (1, 3), (3, 1)])
    above, below = paired(block, block, axis)
    none = jnp.zeros_like(beyond)
    return jnp.concatenate(
        [jnp.where(upper, beyond, none), above, block, below, jnp.where(upper, none, beyond)], axis=1
    )


def taps(field, table, dim, count):
    total = None
    for offset in range(2 * HW + 1):
        shape = [1] * field.ndim
        shape[dim] = count
        term = table[:, offset].reshape(shape) * lax.slice_in_dim(field, offset, offset + count, axis=dim)
        total = term if total is None else total + term
    return total


def flipped(wide, count):
    return jnp.stack([wide[o : o + count, 2 * HW - o] for o in range(2 * HW + 1)], axis=1)


def window(table, axis, count, rim):
    padded = jnp.pad(table, ((rim, rim), (0, 0)))
    return lax.dynamic_slice_in_dim(padded, lax.axis_index(axis) * count, count + 2 * rim, 0)


def body(anomalies, sigma, taper_x, taper_y, taper_z, innovation, obs_inverse, obs_index, obs_slot):
    local_members, slots, cells_x, cells_y, levels = anomalies.shape
    member_devices = lax.axis_size("member")
    ens_weight = 0.8 / math.sqrt(local_members * member_devices - 1)
    share = 1.0 / member_devices
    cells = cells_x * cells_y
    count = obs_index.shape[-1]
    rows = count // levels

    near = 4 if member_devices % 4 == 0 else 1
    far = member_devices // near
    near_groups = groups(member_devices, near, 1)
    far_groups = groups(member_devices, far, near)

    index = obs_index.reshape(1, -1)
    slot = obs_slot.reshape(1, -1)
    obs_weight = obs_inverse.reshape(1, -1)
    first = innovation.reshape(1, -1)

    x_rows_wide = window(taper_x, "sx", cells_x, HW)
    x_rows = x_rows_wide[HW : HW + cells_x]
    x_flip = flipped(x_rows_wide, cells_x)
    y_rows_wide = window(taper_y, "sy", cells_y, HW)
    y_rows = y_rows_wide[HW : HW + cells_y]
    y_flip = flipped(y_rows_wide, cells_y)
    x_pair = jnp.stack([x_rows, x_flip])
    y_pair = jnp.broadcast_to(
        jnp.stack([y_rows.T, y_flip.T])[..., None], (2, 2 * HW + 1, cells_y, levels)
    )

    params = pltpu.CompilerParams(vmem_limit_bytes=40 * 2**20)
    packed = anomalies.reshape(local_members, slots, cells, levels)
    packed_sigma = sigma.reshape(cells, levels)
    side = cells_x * 2 * HW
    wide_y = cells_y + 2 * HW

    whole = pl.BlockSpec(memory_space=pltpu.VMEM)

    def z_products(after):
        table, after = lax.optimization_barrier((taper_z, after))
        return jnp.stack(
            [jnp.dot(table, other, precision=HIGHEST) for other in (table, table.T)]
        ), after

    def apply(first, second, room, z_pair=None):
        stack, low, high = pl.pallas_call(
            functools.partial(adjoint_kernel, ens_weight, cells_y),
            out_shape=(
                jax.ShapeDtypeStruct((local_members + 1, cells, levels), F32),
                jax.ShapeDtypeStruct((local_members + 1, side, levels), F32),
                jax.ShapeDtypeStruct((local_members + 1, side, levels), F32),
            ),
            compiler_params=pltpu.CompilerParams(vmem_limit_bytes=room * 2**20),
        )(slot, index, first, second, packed, packed_sigma)
        left, right = neighbours(low, high, "sy")
        pieces = [
            block.reshape(local_members + 1, cells_x, -1, levels) for block in (left, stack, right)
        ]
        stack = taps(jnp.concatenate(pieces, axis=2), y_rows_wide, 2, wide_y)
        if z_pair is None:
            z_pair, stack = z_products(stack)
        stack = taps(widened(stack, 2 * HW - cells_x, "sx"), x_rows_wide, 1, cells_x + 2 * HW)
        control = stack[:, HW : HW + cells_x, HW : HW + cells_y]
        field, sampled = pl.pallas_call(
            functools.partial(forward_kernel, ens_weight, share),
            out_shape=(
                jax.ShapeDtypeStruct((slots * cells, levels), F32),
                jax.ShapeDtypeStruct((2, count), F32),
            ),
            in_specs=[pl.BlockSpec(memory_space=pltpu.SMEM)] + [whole] * 7,
            scratch_shapes=[
                pltpu.VMEM((local_members + 1, wide_y, levels), F32),
                pltpu.VMEM((local_members + 1, cells, levels), F32),
            ],
            compiler_params=params,
        )(x_pair, slot, index, stack, y_pair, z_pair, packed, packed_sigma)
        return control, field, sampled.reshape(2, rows, levels), z_pair

    control0, field0, sampled0, z_pair = apply(obs_weight, first, 60)
    part = jnp.sum(gathered(sampled0[0], near, "member", near_groups), axis=0)
    seen0 = lax.psum(part, "member", axis_index_groups=far_groups)
    control1, field1, sampled1, _ = apply(obs_weight, seen0.reshape(1, -1), 40, z_pair)

    blocks = (sampled0[1], sampled1[0], sampled1[1], field0, field1)
    flat = jnp.concatenate([block.reshape(near, -1, levels) for block in blocks], axis=1)
    chunk = jnp.sum(exchange(flat, "member", near_groups), axis=0)
    chunk = lax.psum(chunk, "member", axis_index_groups=far_groups)
    total = gathered(chunk, near, "member", near_groups)
    regions = lax.axis_size("sx") * lax.axis_size("sy")
    products = pl.pallas_call(
        product_kernel,
        out_shape=jax.ShapeDtypeStruct((regions, levels), F32),
        compiler_params=params,
    )(total, obs_inverse.reshape(rows, levels), innovation.reshape(rows, levels), seen0)
    products = exchange(products, ("sx", "sy"))
    control, static, increment = pl.pallas_call(
        mix_kernel,
        out_shape=(
            jax.ShapeDtypeStruct((local_members, cells, levels), F32),
            jax.ShapeDtypeStruct((cells, levels), F32),
            jax.ShapeDtypeStruct((slots * cells, levels), F32),
        ),
        compiler_params=params,
    )(
        products,
        control0.reshape(-1, cells, levels),
        control1.reshape(-1, cells, levels),
        taper_z,
        total,
    )
    shape = (cells_x, cells_y, levels)
    return (
        control.reshape((local_members,) + shape),
        static.reshape(shape),
        increment.reshape((slots,) + shape),
    )


def solution(mesh):
    return jax.shard_map(
        body,
        mesh=mesh,
        in_specs=(
            P("member", None, "sx", "sy", None),
            P("sx", "sy", None),
            P(),
            P(),
            P(),
            P("sx", "sy", None),
            P("sx", "sy", None),
            P("sx", "sy", None),
            P("sx", "sy", None),
        ),
        out_specs=(P("member", "sx", "sy", None), P("sx", "sy", None), P(None, "sx", "sy", None)),
        check_vma=False,
    )
```
